32 devices in a mesh: gx: 4 (over z), gy: 4 (over y, core), gz: 2 (over x).
Axes of the slice: x: 2, y: 2, z: 4, core: 2. Of those that a mesh axis runs over, the one named last changes fastest.
Arguments:
- rhs: float32 [128, 128, 256], P('gx', 'gy', 'gz'), may hold values from -8 to 8
- accumulation: float32 [128, 128, 256], P('gx', 'gy', 'gz'), may hold values from 0.05 to 0.5
- permeability: float32 [3, 128, 128, 256], P(None, 'gx', 'gy', 'gz'), may hold values from 0.1 to 10
- nnc_cell: int32 [4, 4, 2, 512], P('gx', 'gy', 'gz'), may hold values from 0 to 4095, as said below
- nnc_remote: int32 [4, 4, 2, 512], P('gx', 'gy', 'gz'), may hold values from 0 to 8191, as said below
- nnc_mask: int32 [4, 4, 2, 512], P('gx', 'gy', 'gz'), may hold values from 0 to 1, as said below
- nnc_trans: float32 [4, 4, 2, 512], P('gx', 'gy', 'gz'), may hold values from 0.5 to 4
Outputs:
- correction: float32 [128, 128, 256], P('gx', 'gy', 'gz')
The draws below stay inside these ranges and needn't reach their ends.
Inputs may be any that keep to these rules, and one draw needn't show every extreme that they name: `nnc_cell`: x * 128 + z of a cell with local x and local layer z on the device's first y layer. `nnc_remote`: x * 256 + z2, with x the same local x as nnc_cell and z2 a global layer, naming a cell on the last y layer of the device below in y. `nnc_mask`: each device's live slots come first, then zeros; every slot is 0 on devices of the first gy index; the device last along every axis has all slots live.
All inputs are finite; a program needn't handle non-finite values.
Results may differ from the reference program's by a relative error of at most 0.00002.
Values sent between devices are 32-bit elements; how exact they have to be, the bound alone decides.
A program may use at most 64 MiB of HBM per device.

```python
import math
import jax
import jax.numpy as jnp

CX = 32
CY = 32
CZ = 128
FSLOT = 512
SWEEPS = 6
TILES_X = 4
TILES_Y = 4
TILES_Z = 2
NX = 128
NY = 128
NZ = 256


def fault_lists(key):
    base = jax.random.fold_in(key, 17)
    keys = jax.random.split(base, 5)
    shape = (TILES_X, TILES_Y, TILES_Z, FSLOT)
    column_x = jax.random.randint(keys[0], shape, 0, CX)
    layer_z = jax.random.randint(keys[1], shape, 0, CZ)
    throw = jax.random.randint(keys[2], (TILES_X, TILES_Y, TILES_Z, 1), -(TILES_Z - 1), TILES_Z)
    jitter = jax.random.randint(keys[3], shape, -(CZ // 2), CZ // 2 + 1)
    tile_z = jnp.arange(TILES_Z, dtype=jnp.int32).reshape(1, 1, TILES_Z, 1)
    remote_z = jnp.clip(tile_z * CZ + layer_z + throw * CZ + jitter, 0, NZ - 1)
    live = jax.random.randint(keys[4], (TILES_X, TILES_Y, TILES_Z, 1), FSLOT // 4, FSLOT + 1)
    live = live.at[TILES_X - 1, TILES_Y - 1, TILES_Z - 1, 0].set(FSLOT)
    tile_y = jnp.arange(TILES_Y, dtype=jnp.int32).reshape(1, TILES_Y, 1, 1)
    slots = jnp.arange(FSLOT, dtype=jnp.int32).reshape(1, 1, 1, FSLOT)
    mask = ((slots < live) & (tile_y > 0)).astype(jnp.int32)
    cells = (column_x * CZ + layer_z).astype(jnp.int32)
    remote = (column_x * NZ + remote_z).astype(jnp.int32)
    return (cells, remote, mask)


def draw_nnc_cell(key, part):
    return fault_lists(key)[0]


def draw_nnc_remote(key, part):
    return fault_lists(key)[1]


def draw_nnc_mask(key, part):
    return fault_lists(key)[2]


def block_scale(stream_key, shape, cuts, low, top_value):
    loudness = 1.0
    for axis_at, parts in cuts:
        steps = jax.random.uniform(jax.random.fold_in(jax.random.fold_in(stream_key, 6), axis_at), (parts,), jnp.float32, low / len(cuts), top_value / len(cuts))
        loudness = loudness * jnp.repeat(jnp.exp(steps), shape[axis_at] // parts).reshape((-1,) + (1,) * (len(shape) - 1 - axis_at))
    return loudness


def normal_values(own_key, extent, width, reach, cuts=(), kind=jnp.bfloat16):
    drawn = width * jax.random.normal(own_key, extent, jnp.float32)
    if cuts:
        drawn = drawn * block_scale(own_key, extent, cuts, -0.22, 0.18)
    return jnp.clip(drawn, -reach, reach).astype(kind)


def setup_inputs(seed: int = 0) -> dict:
    streams_of = jax.random.split(jax.random.key(seed), 8)
    return {
        "rhs": normal_values(streams_of[0], (NX, NY, NZ), 1.0, 8.0, ((0, 4), (1, 4), (2, 2)), jnp.float32),
        "accumulation": jnp.clip(jnp.exp(math.log(0.5) - 2.3025851 * jax.random.uniform(streams_of[1], (NX, NY, NZ), jnp.float32) ** block_scale(streams_of[1], (NX, NY, NZ), ((0, 4), (1, 4), (2, 2)), -0.2, 0.2)), 0.05, 0.5),
        "permeability": jnp.clip(jnp.exp(math.log(10.0) - 4.6051702 * jax.random.uniform(streams_of[2], (3, NX, NY, NZ), jnp.float32) ** block_scale(streams_of[2], (3, NX, NY, NZ), ((1, 4), (2, 4), (3, 2)), -0.2, 0.2)), 0.1, 10.0),
        "nnc_cell": draw_nnc_cell(jax.random.fold_in(streams_of[7], 71), 0),
        "nnc_remote": draw_nnc_remote(jax.random.fold_in(streams_of[7], 71), 0),
        "nnc_mask": draw_nnc_mask(jax.random.fold_in(streams_of[7], 71), 0),
        "nnc_trans": jnp.clip(jnp.exp(math.log(4.0) - 2.0794415 * jax.random.uniform(streams_of[6], (TILES_X, TILES_Y, TILES_Z, FSLOT), jnp.float32) ** block_scale(streams_of[6], (TILES_X, TILES_Y, TILES_Z, FSLOT), ((0, 4), (1, 4), (2, 2)), -0.2, 0.2)), 0.5, 4.0),
    }


lam_low = 0.1
lam_high = 2.0


def harmonic(left, right):
    return 2.0 * (left * right) / (left + right)


def neighbours(padded):
    return (padded[2:, 1:-1, 1:-1], padded[:-2, 1:-1, 1:-1],
            padded[1:-1, 2:, 1:-1], padded[1:-1, :-2, 1:-1],
            padded[1:-1, 1:-1, 2:], padded[1:-1, 1:-1, :-2])


def reference(rhs, accumulation, permeability, nnc_cell, nnc_remote, nnc_mask, nnc_trans):
    padded_perm = jnp.pad(permeability, ((0, 0), (1, 1), (1, 1), (1, 1)))
    transmit = []
    for index in range(6):
        axis_perm = neighbours(padded_perm[index // 2])[index]
        transmit.append(harmonic(permeability[index // 2], axis_perm))
    shape = nnc_cell.shape
    tile_x = jnp.arange(shape[0], dtype=jnp.int32).reshape(-1, 1, 1, 1)
    tile_y = jnp.arange(shape[1], dtype=jnp.int32).reshape(1, -1, 1, 1)
    tile_z = jnp.arange(shape[2], dtype=jnp.int32).reshape(1, 1, -1, 1)
    total = NX * NY * NZ
    cell_a = ((tile_x * CX + nnc_cell // CZ) * NY + tile_y * CY) * NZ + tile_z * CZ + nnc_cell % CZ
    cell_b = ((tile_x * CX + nnc_remote // NZ) * NY + tile_y * CY - 1) * NZ + nnc_remote % NZ
    cell_b = jnp.where(tile_y > 0, cell_b, 0)
    cell_a = cell_a.reshape(-1).astype(jnp.int32)
    cell_b = cell_b.reshape(-1).astype(jnp.int32)
    weight = (nnc_trans * nnc_mask.astype(jnp.float32)).reshape(-1)

    def operate(field):
        beside = neighbours(jnp.pad(field, 1))
        result = accumulation * field
        for index in range(6):
            result = result + transmit[index] * (field - beside[index])
        flat = field.reshape(-1)
        flux = weight * (flat[cell_a] - flat[cell_b])
        extra = jnp.zeros((total,), jnp.float32).at[cell_a].add(flux).at[cell_b].add(-flux)
        return result + extra.reshape(field.shape)

    diag_extra = jnp.zeros((total,), jnp.float32).at[cell_a].add(weight).at[cell_b].add(weight)
    diagonal = accumulation + sum(transmit) + diag_extra.reshape(rhs.shape)
    inverse = 1.0 / diagonal
    theta = (lam_high + lam_low) / 2.0
    delta = (lam_high - lam_low) / 2.0
    sigma = theta / delta
    rho_prev = 1.0 / sigma
    residual = rhs
    direction = inverse * residual / theta
    correction = jnp.zeros_like(rhs)
    for sweep in range(SWEEPS):
        correction = correction + direction
        if sweep < SWEEPS - 1:
            residual = residual - operate(direction)
            rho_next = 1.0 / (2.0 * sigma - rho_prev)
            direction = rho_next * rho_prev * direction + (2.0 * rho_next / delta) * inverse * residual
            rho_prev = rho_next
    return correction
```

```python
import functools
import jax
import jax.numpy as jnp
from jax import lax
from jax.experimental import pallas as pl
from jax.experimental.pallas import tpu as pltpu
from jax.sharding import PartitionSpec as P

SWEEPS = 6
lam_low = 0.1
lam_high = 2.0
F32 = jnp.float32
BF16 = jnp.bfloat16
UNROLL = 4
MESH = pl.DeviceIdType.MESH


def harmonic(left, right):
    return 2.0 * (left * right) / (left + right)


def parts_of(value):
    high = value.astype(BF16).astype(F32)
    rest = value - high
    middle = rest.astype(BF16).astype(F32)
    return high, middle, rest - middle


def stacked(value):
    return jnp.concatenate(parts_of(value), axis=0).astype(BF16)


def one_hot(row, count, kind):
    slots = row.shape[1]
    rows = lax.broadcasted_iota(jnp.int32, (count, slots), 0)
    return jnp.where(rows == row, 1.0, 0.0).astype(kind)


def gathered(face, columns3, layers):
    picked = lax.dot_general(
        stacked(face), columns3, (((0,), (0,)), ((), ())), preferred_element_type=F32
    )
    return jnp.sum(picked * layers, axis=0, keepdims=True)


def scattered(row, columns3, layers):
    depth_x = columns3.shape[0] // 3
    columns = columns3[0:depth_x, :].astype(F32)
    left = jnp.concatenate([columns * part for part in parts_of(row)], axis=0).astype(BF16)
    out = lax.dot_general(left, layers, (((1,), (1,)), ((), ())), preferred_element_type=F32)
    return out[0:depth_x] + out[depth_x : 2 * depth_x] + out[2 * depth_x :]


def kernel(
    sizes, rhs, acc, perm, cell_ref, remote_ref, mask_ref, trans_ref, out,
    c0, c1, inv, g, tx, ty, tz, hy, hyt, hz, hzt,
    ystage, zstage, xland, yland, zland, liststage, listland,
    own_x3, own_z, own_col, up_x3, up_z, up_own,
    xs, xr, ys, yr, zs, zr, ls, lr,
):
    nx, ny, nz = sizes
    dx, dy, dz = rhs.shape
    i, j, l = lax.axis_index("gx"), lax.axis_index("gy"), lax.axis_index("gz")
    column = dz * nz
    if nz == 2:
        z_sides = [((dz - 1) * (1 - l), 1 - l, l >= 0, 0)]
    else:
        z_sides = [(dz - 1, l + 1, l < nz - 1, 0), (0, l - 1, l > 0, 1)]
    x_sides = [(i - 1, i > 0), (i + 1, i < nx - 1)]
    y_sides = [(j - 1, j > 0), (j + 1, j < ny - 1)]

    barrier = pltpu.get_barrier_semaphore()

    def greet(ok, peer):
        @pl.when(ok)
        def _():
            pl.semaphore_signal(barrier, inc=1, device_id=peer, device_id_type=MESH)

        return jnp.where(ok, 1, 0)

    count = 0
    for peer, ok in x_sides:
        count = count + greet(ok, (peer, j, l))
    for peer, ok in y_sides:
        for other in range(nz):
            count = count + greet(ok, (i, peer, other))
    for _, peer, ok, _ in z_sides:
        count = count + greet(ok, (i, j, peer))

    lane = lax.broadcasted_iota(jnp.int32, (dy, dz), 1)
    row = lax.broadcasted_iota(jnp.int32, (dy, dz), 0)

    def pack_shift(x, edge):
        return lax.rem(x + dz - edge, dz)

    def unpack_shift(x, edge):
        return lax.rem(edge + dz - x, dz)

    def pack_into(packs, x, plane):
        return tuple(
            jnp.where(lane == x, pltpu.roll(plane, pack_shift(x, side[0]), 1), p)
            for p, side in zip(packs, z_sides)
        )

    def unpacked(values, x):
        total = 0.0
        for v, side in zip(values, z_sides):
            total = total + jnp.where(
                lane == side[0], pltpu.roll(v, unpack_shift(x, side[0]), 1), 0.0
            )
        return total

    zero_packs = tuple(jnp.zeros((dy, dz), F32) for _ in z_sides)

    def planes(body, carry):
        def step(s, carry):
            for u in range(UNROLL):
                carry = body(s * UNROLL + u, carry)
            return carry

        return lax.fori_loop(0, dx // UNROLL, step, carry)

    def copies(e, x_src):
        sends, receives = [], []
        for side in range(2):
            peer, ok = x_sides[side]
            sends.append((ok, pltpu.make_async_remote_copy(
                x_src[side], xland.at[e, 1 - side], xs.at[e, side], xr.at[e, 1 - side],
                device_id=(peer, j, l), device_id_type=MESH)))
            receives.append((ok, pltpu.make_async_remote_copy(
                x_src[side], xland.at[e, side], xs.at[e, side], xr.at[e, side],
                device_id=(peer, j, l), device_id_type=MESH)))
        for side in range(2):
            peer, ok = y_sides[side]
            for other in range(nz):
                sends.append((ok, pltpu.make_async_remote_copy(
                    ystage.at[e, side], yland.at[e, 1 - side, l],
                    ys.at[e, side, other], yr.at[e, 1 - side, l],
                    device_id=(i, peer, other), device_id_type=MESH)))
                receives.append((ok, pltpu.make_async_remote_copy(
                    ystage.at[e, side], yland.at[e, side, other],
                    ys.at[e, side, other], yr.at[e, side, other],
                    device_id=(i, peer, other), device_id_type=MESH)))
        for _, peer, ok, side in z_sides:
            far = side if len(z_sides) == 1 else 1 - side
            sends.append((ok, pltpu.make_async_remote_copy(
                zstage.at[e, side], zland.at[e, far], zs.at[e, side], zr.at[e, far],
                device_id=(i, j, peer), device_id_type=MESH)))
            receives.append((ok, pltpu.make_async_remote_copy(
                zstage.at[e, side], zland.at[e, side], zs.at[e, side], zr.at[e, side],
                device_id=(i, j, peer), device_id_type=MESH)))
        return sends, receives

    def each(pairs, act):
        for ok, copy in pairs:
            @pl.when(ok)
            def _(copy=copy):
                act(copy)

    cell, remote = cell_ref[...], remote_ref[...]
    weight = trans_ref[...] * mask_ref[...].astype(F32)
    slots = cell.shape[1]
    liststage[...] = jnp.zeros_like(liststage)
    liststage[0:1, :] = cell.astype(F32)
    liststage[1:2, :] = remote.astype(F32)
    liststage[2:3, :] = weight

    def first(x, packs):
        ystage[0, 0, pl.ds(x, 1), :] = perm[1, x, 0:1, :]
        ystage[0, 1, pl.ds(x, 1), :] = perm[1, x, dy - 1 : dy, :]
        return pack_into(packs, x, perm[2, x])

    packs = planes(first, zero_packs)
    for side, p in enumerate(packs):
        zstage[0, side] = p

    for side in range(2):
        @pl.when(jnp.logical_not(x_sides[side][1]))
        def _(side=side):
            for e in range(SWEEPS):
                xland[e, side] = jnp.zeros((dy, dz), F32)

        @pl.when(jnp.logical_not(y_sides[side][1]))
        def _(side=side):
            for e in range(SWEEPS):
                for other in range(nz):
                    yland[e, side, other] = jnp.zeros((dx, dz), F32)
            if side == 1:
                listland[...] = jnp.zeros_like(listland)
    if nz != 2:
        for _, _, ok, side in z_sides:
            @pl.when(jnp.logical_not(ok))
            def _(side=side):
                for e in range(SWEEPS):
                    zland[e, side] = jnp.zeros((dy, dz), F32)

    pl.semaphore_wait(barrier, count)
    sends, receives = copies(0, (perm.at[0, 0], perm.at[0, dx - 1]))
    for other in range(nz):
        sends.append((y_sides[0][1], pltpu.make_async_remote_copy(
            liststage, listland.at[l], ls.at[other], lr.at[l],
            device_id=(i, j - 1, other), device_id_type=MESH)))
        receives.append((y_sides[1][1], pltpu.make_async_remote_copy(
            liststage, listland.at[other], ls.at[other], lr.at[other],
            device_id=(i, j + 1, other), device_id_type=MESH)))
    each(sends, lambda copy: copy.start())
    pending = sends

    shift_z, shift_c = dz.bit_length() - 1, column.bit_length() - 1
    own_rows = one_hot(cell >> shift_z, dx, F32)
    own_x3[...] = jnp.concatenate([own_rows] * 3, axis=0).astype(BF16)
    own_z[...] = one_hot(cell & (dz - 1), dz, BF16)
    own_col[...] = one_hot(remote & (column - 1), column, F32)
    near = scattered(weight, own_x3[...], own_z[...])

    def inner(x, carry):
        @pl.when(x < dx - 1)
        def _():
            tx[x + 1] = harmonic(perm[0, x], perm[0, x + 1])

        k = perm[1, x]
        ty[x] = jnp.where(row == dy - 1, 0.0, harmonic(k, pltpu.roll(k, dy - 1, 0)))
        k = perm[2, x]
        tz[x] = jnp.where(lane == dz - 1, 0.0, harmonic(k, pltpu.roll(k, dz - 1, 1)))
        return carry

    lax.fori_loop(0, dx, inner, 0)

    each(receives, lambda copy: copy.wait_recv())
    tx[0] = harmonic(perm[0, 0], xland[0, 0])
    tx[dx] = harmonic(perm[0, dx - 1], xland[0, 1])
    up_rows = []
    far = 0.0
    for other in range(nz):
        up_cell = listland[other, 0:1, :].astype(jnp.int32)
        up_remote = listland[other, 1:2, :].astype(jnp.int32)
        up_weight = listland[other, 2:3, :]
        rows = one_hot(up_cell >> shift_z, dx, F32)
        up_x3[other] = jnp.concatenate([rows] * 3, axis=0).astype(BF16)
        up_z[other] = one_hot(up_cell & (dz - 1), dz, F32)
        up_own[other] = one_hot((up_remote & (column - 1)) - l * dz, dz, BF16)
        far = far + scattered(up_weight, up_x3[other], up_own[other])
    for side, extra in ((0, near), (1, far)):
        value = 0.0
        for other in range(nz):
            value = jnp.where(l == other, yland[0, side, other], value)
        t = harmonic(ystage[0, side], value)
        hyt[side] = t
        hy[side] = t + extra
    ztotal = []
    for side in range(len(z_sides)):
        t = harmonic(zstage[0, side], zland[0, side])
        hzt[side] = t
        ztotal.append(t)

    theta = (lam_high + lam_low) / 2.0
    delta = (lam_high - lam_low) / 2.0
    sigma = theta / delta

    def faced(x):
        return jnp.where(row == 0, hy[0, pl.ds(x, 1), :], 0.0) + jnp.where(
            row == dy - 1, hy[1, pl.ds(x, 1), :], 0.0
        )

    def stage(e, x, plane, packs):
        ystage[e, 0, pl.ds(x, 1), :] = plane[0:1, :]
        ystage[e, 1, pl.ds(x, 1), :] = plane[dy - 1 : dy, :]
        return pack_into(packs, x, plane)

    def begin(x, packs):
        y, z = ty[x], tz[x]
        diagonal = acc[x] + (tx[x] + tx[x + 1]) + (y + pltpu.roll(y, 1, 0))
        diagonal = diagonal + (z + pltpu.roll(z, 1, 1)) + faced(x) + unpacked(ztotal, x)
        inverse = 1.0 / diagonal
        value = inverse * rhs[x]
        inv[x] = inverse
        g[x] = value
        value = value / theta
        c0[x + 1] = value
        return stage(1, x, value, packs)

    packs = planes(begin, zero_packs)
    now, before = c0, c1
    rho = 1.0 / sigma
    for e in range(1, SWEEPS):
        each(pending, lambda copy: copy.wait_send())
        for side, p in enumerate(packs):
            zstage[e, side] = p
        sends, receives = copies(e, (now.at[1], now.at[dx]))
        each(sends, lambda copy: copy.start())
        pending = sends
        each(receives, lambda copy: copy.wait_recv())
        now[0] = xland[e, 0]
        now[dx + 1] = xland[e, 1]
        flux = 0.0
        far = 0.0
        sides = [0.0, 0.0]
        for other in range(nz):
            rows = slice(other * dz, (other + 1) * dz)
            flux = flux + gathered(yland[e, 0, other], own_x3[...], own_col[rows, :])
            up = listland[other, 2:3, :] * gathered(yland[e, 1, other], up_x3[other], up_z[other])
            far = far + scattered(up, up_x3[other], up_own[other])
            for side in range(2):
                sides[side] = jnp.where(l == other, yland[e, side, other], sides[side])
        near = scattered(weight * flux, own_x3[...], own_z[...])
        hy[0] = hyt[0] * sides[0] + near
        hy[1] = hyt[1] * sides[1] + far
        zvalues = [hzt[side] * zland[e, side] for side in range(len(z_sides))]

        rho_next = 1.0 / (2.0 * sigma - rho)
        a, b = rho_next * rho, 2.0 * rho_next / delta
        rho = rho_next

        def sweep(x, packs, e=e, now=now, before=before, a=a, b=b, zvalues=zvalues):
            v = now[x + 1]
            y, z = ty[x], tz[x]
            total = tx[x + 1] * now[x + 2] + tx[x] * now[x]
            total = total + (y * pltpu.roll(v, dy - 1, 0) + pltpu.roll(y * v, 1, 0))
            total = total + (z * pltpu.roll(v, dz - 1, 1) + pltpu.roll(z * v, 1, 1))
            total = total + faced(x) + unpacked(zvalues, x)
            new = (1.0 + a - b) * v + b * (g[x] + inv[x] * total)
            if e > 1:
                new = new - a * before[x + 1]
            if e == SWEEPS - 1:
                out[x] = new
                return packs
            before[x + 1] = new
            return stage(e + 1, x, new, packs)

        packs = planes(sweep, zero_packs)
        now, before = before, now
    each(pending, lambda copy: copy.wait_send())


def local(sizes, rhs, accumulation, permeability, nnc_cell, nnc_remote, nnc_mask, nnc_trans):
    nx, ny, nz = sizes
    dx, dy, dz = rhs.shape
    slots = nnc_cell.shape[-1]
    column = dz * nz
    plane = (dx, dy, dz)
    zn = 1 if nz == 2 else 2
    vmem = pl.BlockSpec(memory_space=pltpu.VMEM)
    dma = pltpu.SemaphoreType.DMA
    V = pltpu.VMEM
    scratch = [
        V((dx + 2, dy, dz), F32), V((dx + 2, dy, dz), F32),
        V(plane, F32), V(plane, F32),
        V((dx + 1, dy, dz), F32), V(plane, F32), V(plane, F32),
        V((2, dx, dz), F32), V((2, dx, dz), F32),
        V((zn, dy, dz), F32), V((zn, dy, dz), F32),
        V((SWEEPS, 2, dx, dz), F32), V((SWEEPS, zn, dy, dz), F32),
        V((SWEEPS, 2, dy, dz), F32), V((SWEEPS, 2, nz, dx, dz), F32),
        V((SWEEPS, zn, dy, dz), F32),
        V((8, slots), F32), V((nz, 8, slots), F32),
        V((3 * dx, slots), BF16), V((dz, slots), BF16), V((column, slots), F32),
        V((nz, 3 * dx, slots), BF16), V((nz, dz, slots), F32), V((nz, dz, slots), BF16),
        dma((SWEEPS, 2)), dma((SWEEPS, 2)),
        dma((SWEEPS, 2, nz)), dma((SWEEPS, 2, nz)),
        dma((SWEEPS, zn)), dma((SWEEPS, zn)),
        dma((nz,)), dma((nz,)),
    ]
    return pl.pallas_call(
        functools.partial(kernel, sizes),
        out_shape=jax.ShapeDtypeStruct(plane, F32),
        in_specs=[vmem] * 7,
        out_specs=vmem,
        scratch_shapes=scratch,
        compiler_params=pltpu.CompilerParams(
            collective_id=0, has_side_effects=True, vmem_limit_bytes=48 * 1024 * 1024
        ),
    )(
        rhs, accumulation, permeability,
        *(v.reshape(1, slots) for v in (nnc_cell, nnc_remote, nnc_mask, nnc_trans)),
    )


def solution(mesh):
    sizes = tuple(mesh.shape[name] for name in ("gx", "gy", "gz"))
    cells = P("gx", "gy", "gz")
    lists = P("gx", "gy", "gz", None)
    return jax.shard_map(
        functools.partial(local, sizes),
        mesh=mesh,
        in_specs=(cells, cells, P(None, "gx", "gy", "gz"), lists, lists, lists, lists),
        out_specs=cells,
        check_vma=False,
    )
```

```python
import functools
import jax
import jax.numpy as jnp
from jax import lax
from jax.experimental import pallas as pl
from jax.experimental.pallas import tpu as pltpu
from jax.sharding import PartitionSpec as P

SWEEPS = 6
lam_low = 0.1
lam_high = 2.0
F32 = jnp.float32
BF16 = jnp.bfloat16
UNROLL = 4
MESH = pl.DeviceIdType.MESH


def harmonic(left, right):
    return 2.0 * (left * right) / (left + right)


def parts_of(value):
    high = value.astype(BF16).astype(F32)
    rest = value - high
    middle = rest.astype(BF16).astype(F32)
    return high, middle, rest - middle


def stacked(value):
    return jnp.concatenate(parts_of(value), axis=0).astype(BF16)


def one_hot(row, count, kind):
    slots = row.shape[1]
    rows = lax.broadcasted_iota(jnp.int32, (count, slots), 0)
    return jnp.where(rows == row, 1.0, 0.0).astype(kind)


def gathered(face, columns3, layers):
    picked = lax.dot_general(
        stacked(face), columns3, (((0,), (0,)), ((), ())), preferred_element_type=F32
    )
    return jnp.sum(picked * layers, axis=0, keepdims=True)


def scattered(row, columns3, layers):
    depth_x = columns3.shape[0] // 3
    columns = columns3[0:depth_x, :].astype(F32)
    left = jnp.concatenate([columns * part for part in parts_of(row)], axis=0).astype(BF16)
    out = lax.dot_general(left, layers, (((1,), (1,)), ((), ())), preferred_element_type=F32)
    return out[0:depth_x] + out[depth_x : 2 * depth_x] + out[2 * depth_x :]


def kernel(
    sizes, rhs_in, acc_in, perm_in, cell_in, remote_in, mask_in, trans_in, out,
    rhs, acc, perm, cell_ref, remote_ref, mask_ref, trans_ref, load,
    c0, c1, inv, g, tx, ty, tz, hx, hxt, hy, hyt, hz, hzt, yinv, zinv, ypart, turn,
    xstage, ystage, zstage, xland, yland, zland, liststage, listland,
    own_x3, own_z, own_col, up_x3, up_z, up_own,
    xs, xr, ys, yr, zs, zr, ls, lr,
):
    nx, ny, nz = sizes
    dx, dy, dz = rhs.shape
    i, j, l = lax.axis_index("gx"), lax.axis_index("gy"), lax.axis_index("gz")
    column = dz * nz
    if nz == 2:
        z_sides = [((dz - 1) * (1 - l), 1 - l, l >= 0, 0)]
    else:
        z_sides = [(dz - 1, l + 1, l < nz - 1, 0), (0, l - 1, l > 0, 1)]
    x_sides = [(i - 1, i > 0), (i + 1, i < nx - 1)]
    y_sides = [(j - 1, j > 0), (j + 1, j < ny - 1)]

    loads = [
        pltpu.make_async_copy(src, dst, load.at[index])
        for index, (src, dst) in enumerate((
            (cell_in, cell_ref), (remote_in, remote_ref), (mask_in, mask_ref),
            (trans_in, trans_ref), (perm_in, perm), (acc_in, acc), (rhs_in, rhs)))
    ]
    for copy in loads:
        copy.start()

    barrier = pltpu.get_barrier_semaphore()

    def greet(ok, peer):
        @pl.when(ok)
        def _():
            pl.semaphore_signal(barrier, inc=1, device_id=peer, device_id_type=MESH)

        return jnp.where(ok, 1, 0)

    count = 0
    for peer, ok in x_sides:
        count = count + greet(ok, (peer, j, l))
    for peer, ok in y_sides:
        for other in range(nz):
            count = count + greet(ok, (i, peer, other))
    for _, peer, ok, _ in z_sides:
        count = count + greet(ok, (i, j, peer))

    lane = lax.broadcasted_iota(jnp.int32, (dy, dz), 1)
    row = lax.broadcasted_iota(jnp.int32, (dy, dz), 0)

    def pack_shift(x, edge):
        return lax.rem(x + dz - edge, dz)

    def unpack_shift(x, edge):
        return lax.rem(edge + dz - x, dz)

    def pack_into(packs, x, plane):
        return tuple(
            jnp.where(lane == x, pltpu.roll(plane, pack_shift(x, side[0]), 1), p)
            for p, side in zip(packs, z_sides)
        )

    def unpacked(values, x):
        total = 0.0
        for v, side in zip(values, z_sides):
            total = total + jnp.where(
                lane == side[0], pltpu.roll(v, unpack_shift(x, side[0]), 1), 0.0
            )
        return total

    zero_packs = tuple(jnp.zeros((dy, dz), F32) for _ in z_sides)

    def planes(body, carry):
        def step(s, carry):
            for u in range(UNROLL):
                carry = body(s * UNROLL + u, carry)
            return carry

        return lax.fori_loop(0, dx // UNROLL, step, carry)

    def copies(e, x_src):
        sends, receives = [], []
        for side in range(2):
            peer, ok = x_sides[side]
            sends.append((ok, pltpu.make_async_remote_copy(
                x_src[side], xland.at[e, 1 - side], xs.at[e, side], xr.at[e, 1 - side],
                device_id=(peer, j, l), device_id_type=MESH)))
            receives.append((ok, pltpu.make_async_remote_copy(
                x_src[side], xland.at[e, side], xs.at[e, side], xr.at[e, side],
                device_id=(peer, j, l), device_id_type=MESH)))
        for side in range(2):
            peer, ok = y_sides[side]
            for other in range(nz):
                sends.append((ok, pltpu.make_async_remote_copy(
                    ystage.at[e, side], yland.at[e, 1 - side, l],
                    ys.at[e, side, other], yr.at[e, 1 - side, l],
                    device_id=(i, peer, other), device_id_type=MESH)))
                receives.append((ok, pltpu.make_async_remote_copy(
                    ystage.at[e, side], yland.at[e, side, other],
                    ys.at[e, side, other], yr.at[e, side, other],
                    device_id=(i, peer, other), device_id_type=MESH)))
        for _, peer, ok, side in z_sides:
            far = side if len(z_sides) == 1 else 1 - side
            sends.append((ok, pltpu.make_async_remote_copy(
                zstage.at[e, side], zland.at[e, far], zs.at[e, side], zr.at[e, far],
                device_id=(i, j, peer), device_id_type=MESH)))
            receives.append((ok, pltpu.make_async_remote_copy(
                zstage.at[e, side], zland.at[e, side], zs.at[e, side], zr.at[e, side],
                device_id=(i, j, peer), device_id_type=MESH)))
        return sends, receives

    def each(pairs, act):
        for ok, copy in pairs:
            @pl.when(ok)
            def _(copy=copy):
                act(copy)

    for copy in loads[:4]:
        copy.wait()
    cell, remote = cell_ref[...], remote_ref[...]
    weight = trans_ref[...] * mask_ref[...].astype(F32)
    slots = cell.shape[1]
    liststage[...] = jnp.zeros_like(liststage)
    liststage[0:1, :] = cell.astype(F32)
    liststage[1:2, :] = remote.astype(F32)
    liststage[2:3, :] = weight

    for ref in (c0, c1):
        ref[0] = jnp.zeros((dy, dz), F32)
        ref[dx + 1] = jnp.zeros((dy, dz), F32)
    loads[4].wait()

    def first(x, packs):
        ystage[0, 0, pl.ds(x, 1), :] = perm[1, x, 0:1, :]
        ystage[0, 1, pl.ds(x, 1), :] = perm[1, x, dy - 1 : dy, :]
        return pack_into(packs, x, perm[2, x])

    packs = planes(first, zero_packs)
    for side, p in enumerate(packs):
        zstage[0, side] = p

    for side in range(2):
        @pl.when(jnp.logical_not(x_sides[side][1]))
        def _(side=side):
            for e in range(SWEEPS):
                xland[e, side] = jnp.zeros((dy, dz), F32)

        @pl.when(jnp.logical_not(y_sides[side][1]))
        def _(side=side):
            for e in range(SWEEPS):
                for other in range(nz):
                    yland[e, side, other] = jnp.zeros((dx, dz), F32)
            if side == 1:
                listland[...] = jnp.zeros_like(listland)
    if nz != 2:
        for _, _, ok, side in z_sides:
            @pl.when(jnp.logical_not(ok))
            def _(side=side):
                for e in range(SWEEPS):
                    zland[e, side] = jnp.zeros((dy, dz), F32)

    pl.semaphore_wait(barrier, count)
    sends, receives = copies(0, (perm.at[0, 0], perm.at[0, dx - 1]))
    for other in range(nz):
        sends.append((y_sides[0][1], pltpu.make_async_remote_copy(
            liststage, listland.at[l], ls.at[other], lr.at[l],
            device_id=(i, j - 1, other), device_id_type=MESH)))
        receives.append((y_sides[1][1], pltpu.make_async_remote_copy(
            liststage, listland.at[other], ls.at[other], lr.at[other],
            device_id=(i, j + 1, other), device_id_type=MESH)))
    each(sends, lambda copy: copy.start())
    pending = sends

    shift_z, shift_c = dz.bit_length() - 1, column.bit_length() - 1
    own_rows = one_hot(cell >> shift_z, dx, F32)
    own_x3[...] = jnp.concatenate([own_rows] * 3, axis=0).astype(BF16)
    own_z[...] = one_hot(cell & (dz - 1), dz, BF16)
    own_col[...] = one_hot(remote & (column - 1), column, F32)
    near = scattered(weight, own_x3[...], own_z[...])

    def inner(x, carry):
        @pl.when(x < dx - 1)
        def _():
            tx[x + 1] = harmonic(perm[0, x], perm[0, x + 1])

        k = perm[1, x]
        ty[x] = jnp.where(row == dy - 1, 0.0, harmonic(k, pltpu.roll(k, dy - 1, 0)))
        k = perm[2, x]
        tz[x] = jnp.where(lane == dz - 1, 0.0, harmonic(k, pltpu.roll(k, dz - 1, 1)))
        return carry

    lax.fori_loop(0, dx, inner, 0)

    each(receives, lambda copy: copy.wait_recv())
    for copy in loads[5:]:
        copy.wait()
    tx[0] = harmonic(perm[0, 0], xland[0, 0])
    tx[dx] = harmonic(perm[0, dx - 1], xland[0, 1])
    up_rows = []
    far = 0.0
    for other in range(nz):
        up_cell = listland[other, 0:1, :].astype(jnp.int32)
        up_remote = listland[other, 1:2, :].astype(jnp.int32)
        up_weight = listland[other, 2:3, :]
        rows = one_hot(up_cell >> shift_z, dx, F32)
        up_x3[other] = jnp.concatenate([rows] * 3, axis=0).astype(BF16)
        up_z[other] = one_hot(up_cell & (dz - 1), dz, F32)
        up_own[other] = one_hot((up_remote & (column - 1)) - l * dz, dz, BF16)
        far = far + scattered(up_weight, up_x3[other], up_own[other])
    for side, extra in ((0, near), (1, far)):
        value = 0.0
        for other in range(nz):
            value = jnp.where(l == other, yland[0, side, other], value)
        t = harmonic(ystage[0, side], value)
        hyt[side] = t
        hy[side] = t + extra
    ztotal = []
    for side in range(len(z_sides)):
        t = jnp.where(lane < dx, harmonic(zstage[0, side], zland[0, side]), 0.0)
        hzt[side] = t
        ztotal.append(t)

    theta = (lam_high + lam_low) / 2.0
    delta = (lam_high - lam_low) / 2.0
    sigma = theta / delta

    def faced(x):
        return jnp.where(row == 0, hy[0, pl.ds(x, 1), :], 0.0) + jnp.where(
            row == dy - 1, hy[1, pl.ds(x, 1), :], 0.0
        )

    def rims(x, values):
        return faced(x) + unpacked(values, x)

    def put_rows(ref, x, plane):
        ref[0, pl.ds(x, 1), :] = plane[0:1, :]
        ref[1, pl.ds(x, 1), :] = plane[dy - 1 : dy, :]

    def begin(x, carry):
        packs, inv_packs = carry
        y, z = ty[x], tz[x]
        diagonal = acc[x] + (tx[x] + tx[x + 1]) + (y + pltpu.roll(y, 1, 0))
        diagonal = diagonal + (z + pltpu.roll(z, 1, 1)) + rims(x, ztotal)
        inverse = 1.0 / diagonal
        value = inverse * rhs[x]
        inv[x] = inverse
        g[x] = value
        value = value / theta
        c0[x + 1] = value
        put_rows(ystage.at[1], x, value)
        put_rows(yinv, x, inverse)
        return pack_into(packs, x, value), pack_into(inv_packs, x, inverse)

    packs, inv_packs = planes(begin, (zero_packs, zero_packs))
    for side in range(len(z_sides)):
        zstage[1, side] = packs[side]
        zinv[side] = inv_packs[side]
    xstage[1, 0] = c0[1]
    xstage[1, 1] = c0[dx]
    for side, edge in ((0, 0), (1, dx)):
        hxt[side] = tx[edge]
        tx[edge] = jnp.zeros((dy, dz), F32)

    square = dz - 2 * dx
    now, before = c0, c1
    rho = 1.0 / sigma
    b = 0.0
    for e in range(1, SWEEPS):
        each(pending, lambda copy: copy.wait_send())
        sends, receives = copies(e, (xstage.at[e, 0], xstage.at[e, 1]))
        each(sends, lambda copy: copy.start())
        pending = sends

        rho_next = 1.0 / (2.0 * sigma - rho)
        a, b_old, b = rho_next * rho, b, 2.0 * rho_next / delta
        rho = rho_next
        if e > 1:
            now[1] = xstage[e, 0]
            now[dx] = xstage[e, 1]

        def bulk(x, packs, fix, e=e, now=now, before=before, a=a, b=b, b_old=b_old):
            if fix and e > 1:
                values = [hz[side] for side in range(len(z_sides))]
                now[x + 2] = now[x + 2] + b_old * inv[x + 1] * rims(x + 1, values)
            v = now[x + 1]
            y, z = ty[x], tz[x]
            total = tx[x + 1] * now[x + 2] + tx[x] * now[x]
            total = total + (y * pltpu.roll(v, dy - 1, 0) + pltpu.roll(y * v, 1, 0))
            total = total + (z * pltpu.roll(v, dz - 1, 1) + pltpu.roll(z * v, 1, 1))
            new = (1.0 + a - b) * v + b * (g[x] + inv[x] * total)
            if e > 1:
                new = new - a * before[x + 1]
            before[x + 1] = new
            if e == SWEEPS - 1:
                return packs
            put_rows(ypart, x, new)
            return pack_into(packs, x, new)

        def group(step, packs, bulk=bulk):
            for u in range(UNROLL):
                packs = bulk(step * UNROLL + u, packs, True)
            return packs

        packs = lax.fori_loop(0, dx // UNROLL - 1, group, zero_packs)
        for x in range(dx - UNROLL, dx):
            packs = bulk(x, packs, x < dx - 2)

        each(receives, lambda copy: copy.wait_recv())
        flux = 0.0
        far = 0.0
        sides = [0.0, 0.0]
        for other in range(nz):
            rows = slice(other * dz, (other + 1) * dz)
            flux = flux + gathered(yland[e, 0, other], own_x3[...], own_col[rows, :])
            up = listland[other, 2:3, :] * gathered(yland[e, 1, other], up_x3[other], up_z[other])
            far = far + scattered(up, up_x3[other], up_own[other])
            for side in range(2):
                sides[side] = jnp.where(l == other, yland[e, side, other], sides[side])
        near = scattered(weight * flux, own_x3[...], own_z[...])
        yvalues = [hyt[0] * sides[0] + near, hyt[1] * sides[1] + far]
        for side in range(2):
            hy[side] = yvalues[side]
            hx[side] = hxt[side] * xland[e, side]
        zvalues = [hzt[side] * zland[e, side] for side in range(len(z_sides))]
        for side in range(len(z_sides)):
            hz[side] = zvalues[side]

        ends = []
        for side, x in ((0, 0), (1, dx - 1)):
            ends.append(before[x + 1] + b * inv[x] * (hx[side] + rims(x, zvalues)))
        if e == SWEEPS - 1:
            out[0] = ends[0]
            out[dx - 1] = ends[1]

            def last(x, carry, before=before, b=b):
                values = [hz[side] for side in range(len(z_sides))]
                out[x] = before[x + 1] + b * inv[x] * rims(x, values)
                return carry

            lax.fori_loop(1, dx - 1, last, 0)
            continue
        xstage[e + 1, 0] = ends[0]
        xstage[e + 1, 1] = ends[1]
        xrow = lax.broadcasted_iota(jnp.int32, (dx, dz), 0)
        xlane = lax.broadcasted_iota(jnp.int32, (dx, dz), 1)
        turned = [
            jnp.concatenate([v, jnp.zeros((dz - dy, dz), F32)], axis=0).T[0:dx, :]
            for v in zvalues
        ]
        for side, y in ((0, 0), (1, dy - 1)):
            term = yvalues[side]
            term = term + jnp.where(xrow == 0, hx[0, y : y + 1, :], 0.0)
            term = term + jnp.where(xrow == dx - 1, hx[1, y : y + 1, :], 0.0)
            for t, (edge, _, _, _) in zip(turned, z_sides):
                shifted = pltpu.roll(t, lax.rem(edge + dz - y, dz), 1)
                term = term + jnp.where(xlane == edge, shifted, 0.0)
            ystage[e + 1, side] = ypart[side] + b * yinv[side] * term
        turn[...] = jnp.concatenate(yvalues + [jnp.zeros((square, dz), F32)], axis=0).T
        for (edge, _, _, zside), p in zip(z_sides, packs):
            line = turn[pl.ds(edge, 1), :]
            line = jnp.broadcast_to(line, (8, dz))
            upper = pltpu.roll(line, dz - dx, 1)
            term = zvalues[zside]
            term = term + jnp.where(row == 0, line[0:1, :], 0.0)
            term = term + jnp.where(row == dy - 1, upper[0:1, :], 0.0)
            for side, x in ((0, 0), (1, dx - 1)):
                shifted = pltpu.roll(hx[side], pack_shift(x, edge), 1)
                term = term + jnp.where(lane == x, shifted, 0.0)
            zstage[e + 1, zside] = p + b * zinv[zside] * term
        now, before = before, now
    each(pending, lambda copy: copy.wait_send())


def local(sizes, rhs, accumulation, permeability, nnc_cell, nnc_remote, nnc_mask, nnc_trans):
    nx, ny, nz = sizes
    dx, dy, dz = rhs.shape
    slots = nnc_cell.shape[-1]
    column = dz * nz
    plane = (dx, dy, dz)
    zn = 1 if nz == 2 else 2
    vmem = pl.BlockSpec(memory_space=pltpu.VMEM)
    hbm = pl.BlockSpec(memory_space=pltpu.HBM)
    dma = pltpu.SemaphoreType.DMA
    V = pltpu.VMEM
    scratch = [
        V(plane, F32), V(plane, F32), V((3, *plane), F32),
        V((1, slots), jnp.int32), V((1, slots), jnp.int32), V((1, slots), jnp.int32),
        V((1, slots), F32), dma((7,)),
        V((dx + 2, dy, dz), F32), V((dx + 2, dy, dz), F32),
        V(plane, F32), V(plane, F32),
        V((dx + 1, dy, dz), F32), V(plane, F32), V(plane, F32),
        V((2, dy, dz), F32), V((2, dy, dz), F32), V((2, dx, dz), F32), V((2, dx, dz), F32),
        V((zn, dy, dz), F32), V((zn, dy, dz), F32),
        V((2, dx, dz), F32), V((zn, dy, dz), F32), V((2, dx, dz), F32), V((dz, dz), F32),
        V((SWEEPS, 2, dy, dz), F32),
        V((SWEEPS, 2, dx, dz), F32), V((SWEEPS, zn, dy, dz), F32),
        V((SWEEPS, 2, dy, dz), F32), V((SWEEPS, 2, nz, dx, dz), F32),
        V((SWEEPS, zn, dy, dz), F32),
        V((8, slots), F32), V((nz, 8, slots), F32),
        V((3 * dx, slots), BF16), V((dz, slots), BF16), V((column, slots), F32),
        V((nz, 3 * dx, slots), BF16), V((nz, dz, slots), F32), V((nz, dz, slots), BF16),
        dma((SWEEPS, 2)), dma((SWEEPS, 2)),
        dma((SWEEPS, 2, nz)), dma((SWEEPS, 2, nz)),
        dma((SWEEPS, zn)), dma((SWEEPS, zn)),
        dma((nz,)), dma((nz,)),
    ]
    return pl.pallas_call(
        functools.partial(kernel, sizes),
        out_shape=jax.ShapeDtypeStruct(plane, F32),
        in_specs=[hbm] * 7,
        out_specs=vmem,
        scratch_shapes=scratch,
        compiler_params=pltpu.CompilerParams(
            collective_id=0, has_side_effects=True, vmem_limit_bytes=48 * 1024 * 1024
        ),
    )(
        rhs, accumulation, permeability,
        *(v.reshape(1, slots) for v in (nnc_cell, nnc_remote, nnc_mask, nnc_trans)),
    )


def solution(mesh):
    sizes = tuple(mesh.shape[name] for name in ("gx", "gy", "gz"))
    cells = P("gx", "gy", "gz")
    lists = P("gx", "gy", "gz", None)
    return jax.shard_map(
        functools.partial(local, sizes),
        mesh=mesh,
        in_specs=(cells, cells, P(None, "gx", "gy", "gz"), lists, lists, lists, lists),
        out_specs=cells,
        check_vma=False,
    )
```

```python
import functools
import jax
import jax.numpy as jnp
from jax import lax
from jax.experimental import pallas as pl
from jax.experimental.pallas import tpu as pltpu
from jax.sharding import PartitionSpec as P

SWEEPS = 6
lam_low = 0.1
lam_high = 2.0
F32 = jnp.float32
BF16 = jnp.bfloat16
UNROLL = 4
MESH = pl.DeviceIdType.MESH


def harmonic(left, right):
    return 2.0 * (left * right) / (left + right)


def parts_of(value):
    high = value.astype(BF16).astype(F32)
    rest = value - high
    middle = rest.astype(BF16).astype(F32)
    return high, middle, rest - middle


def stacked(value):
    return jnp.concatenate(parts_of(value), axis=0).astype(BF16)


def one_hot(row, count, kind):
    slots = row.shape[1]
    rows = lax.broadcasted_iota(jnp.int32, (count, slots), 0)
    return jnp.where(rows == row, 1.0, 0.0).astype(kind)


def gathered(face, columns3, layers):
    picked = lax.dot_general(
        stacked(face), columns3, (((0,), (0,)), ((), ())), preferred_element_type=F32
    )
    return jnp.sum(picked * layers, axis=0, keepdims=True)


def scattered(row, columns3, layers):
    depth_x = columns3.shape[0] // 3
    columns = columns3[0:depth_x, :].astype(F32)
    left = jnp.concatenate([columns * part for part in parts_of(row)], axis=0).astype(BF16)
    out = lax.dot_general(left, layers, (((1,), (1,)), ((), ())), preferred_element_type=F32)
    return out[0:depth_x] + out[depth_x : 2 * depth_x] + out[2 * depth_x :]


def kernel(
    sizes, rhs_in, acc_in, perm_in, cell_in, remote_in, mask_in, trans_in, out,
    rhs, acc, perm, cell_ref, remote_ref, mask_ref, trans_ref, load,
    c0, c1, inv, g, tx, ty, tz, hx, hxt, hy, hyt, hz, hzt, yinv, zinv, ypart, turn,
    xstage, ystage, zstage, xland, yland, zland, liststage, listland,
    own_x3, own_z, own_col, up_x3, up_z, up_own,
    xs, xr, ys, yr, zs, zr, ls, lr,
):
    nx, ny, nz = sizes
    dx, dy, dz = rhs.shape
    i, j, l = lax.axis_index("gx"), lax.axis_index("gy"), lax.axis_index("gz")
    column = dz * nz
    if nz == 2:
        z_sides = [((dz - 1) * (1 - l), 1 - l, l >= 0, 0)]
    else:
        z_sides = [(dz - 1, l + 1, l < nz - 1, 0), (0, l - 1, l > 0, 1)]
    x_sides = [(i - 1, i > 0), (i + 1, i < nx - 1)]
    y_sides = [(j - 1, j > 0), (j + 1, j < ny - 1)]

    loads = [
        pltpu.make_async_copy(src, dst, load.at[index])
        for index, (src, dst) in enumerate((
            (cell_in, cell_ref), (remote_in, remote_ref), (mask_in, mask_ref),
            (trans_in, trans_ref), (perm_in.at[1], perm.at[1]), (perm_in.at[2], perm.at[2]),
            (perm_in.at[0], perm.at[0]), (acc_in, acc), (rhs_in, rhs)))
    ]
    barrier = pltpu.get_barrier_semaphore()

    def greet(ok, peer):
        @pl.when(ok)
        def _():
            pl.semaphore_signal(barrier, inc=1, device_id=peer, device_id_type=MESH)

        return jnp.where(ok, 1, 0)

    count = 0
    for peer, ok in x_sides:
        count = count + greet(ok, (peer, j, l))
    for peer, ok in y_sides:
        for other in range(nz):
            count = count + greet(ok, (i, peer, other))
    for _, peer, ok, _ in z_sides:
        count = count + greet(ok, (i, j, peer))

    for copy in loads:
        copy.start()

    lane = lax.broadcasted_iota(jnp.int32, (dy, dz), 1)
    row = lax.broadcasted_iota(jnp.int32, (dy, dz), 0)

    def pack_shift(x, edge):
        return lax.rem(x + dz - edge, dz)

    def unpack_shift(x, edge):
        return lax.rem(edge + dz - x, dz)

    def pack_into(packs, x, plane):
        return tuple(
            jnp.where(lane == x, pltpu.roll(plane, pack_shift(x, side[0]), 1), p)
            for p, side in zip(packs, z_sides)
        )

    def unpacked(values, x):
        total = 0.0
        for v, side in zip(values, z_sides):
            total = total + jnp.where(
                lane == side[0], pltpu.roll(v, unpack_shift(x, side[0]), 1), 0.0
            )
        return total

    zero_packs = tuple(jnp.zeros((dy, dz), F32) for _ in z_sides)

    def planes(body, carry):
        def step(s, carry):
            for u in range(UNROLL):
                carry = body(s * UNROLL + u, carry)
            return carry

        return lax.fori_loop(0, dx // UNROLL, step, carry)

    def copies(e, x_src):
        sends, receives = ([], [], []), ([], [], [])
        for side in range(2):
            peer, ok = x_sides[side]
            sends[0].append((ok, pltpu.make_async_remote_copy(
                x_src[side], xland.at[e, 1 - side], xs.at[e, side], xr.at[e, 1 - side],
                device_id=(peer, j, l), device_id_type=MESH)))
            receives[0].append((ok, pltpu.make_async_remote_copy(
                x_src[side], xland.at[e, side], xs.at[e, side], xr.at[e, side],
                device_id=(peer, j, l), device_id_type=MESH)))
        for side in range(2):
            peer, ok = y_sides[side]
            for other in range(nz):
                sends[1].append((ok, pltpu.make_async_remote_copy(
                    ystage.at[e, side], yland.at[e, 1 - side, l],
                    ys.at[e, side, other], yr.at[e, 1 - side, l],
                    device_id=(i, peer, other), device_id_type=MESH)))
                receives[1].append((ok, pltpu.make_async_remote_copy(
                    ystage.at[e, side], yland.at[e, side, other],
                    ys.at[e, side, other], yr.at[e, side, other],
                    device_id=(i, peer, other), device_id_type=MESH)))
        for _, peer, ok, side in z_sides:
            far = side if len(z_sides) == 1 else 1 - side
            sends[2].append((ok, pltpu.make_async_remote_copy(
                zstage.at[e, side], zland.at[e, far], zs.at[e, side], zr.at[e, far],
                device_id=(i, j, peer), device_id_type=MESH)))
            receives[2].append((ok, pltpu.make_async_remote_copy(
                zstage.at[e, side], zland.at[e, side], zs.at[e, side], zr.at[e, side],
                device_id=(i, j, peer), device_id_type=MESH)))
        return sends, receives

    def each(pairs, act):
        for ok, copy in pairs:
            @pl.when(ok)
            def _(copy=copy):
                act(copy)

    for copy in loads[:4]:
        copy.wait()
    cell, remote = cell_ref[...], remote_ref[...]
    weight = trans_ref[...] * mask_ref[...].astype(F32)
    slots = cell.shape[1]
    liststage[...] = jnp.zeros_like(liststage)
    liststage[0:1, :] = cell.astype(F32)
    liststage[1:2, :] = remote.astype(F32)
    liststage[2:3, :] = weight

    for ref in (c0, c1):
        ref[0] = jnp.zeros((dy, dz), F32)
        ref[dx + 1] = jnp.zeros((dy, dz), F32)

    for side in range(2):
        @pl.when(jnp.logical_not(x_sides[side][1]))
        def _(side=side):
            for e in range(SWEEPS):
                xland[e, side] = jnp.zeros((dy, dz), F32)

        @pl.when(jnp.logical_not(y_sides[side][1]))
        def _(side=side):
            for e in range(SWEEPS):
                for other in range(nz):
                    yland[e, side, other] = jnp.zeros((dx, dz), F32)
            if side == 1:
                listland[...] = jnp.zeros_like(listland)
    if nz != 2:
        for _, _, ok, side in z_sides:
            @pl.when(jnp.logical_not(ok))
            def _(side=side):
                for e in range(SWEEPS):
                    zland[e, side] = jnp.zeros((dy, dz), F32)

    pl.semaphore_wait(barrier, count)

    def start(copy):
        copy.start()

    pending = []
    list_sends, list_receives = [], []
    for other in range(nz):
        list_sends.append((y_sides[0][1], pltpu.make_async_remote_copy(
            liststage, listland.at[l], ls.at[other], lr.at[l],
            device_id=(i, j - 1, other), device_id_type=MESH)))
        list_receives.append((y_sides[1][1], pltpu.make_async_remote_copy(
            liststage, listland.at[other], ls.at[other], lr.at[other],
            device_id=(i, j + 1, other), device_id_type=MESH)))
    each(list_sends, start)
    pending += list_sends
    sends, receives = copies(0, (perm_in.at[0, 0], perm_in.at[0, dx - 1]))
    each(sends[0], start)

    for copy in loads[4:6]:
        copy.wait()

    def first(x, packs):
        ystage[0, 0, pl.ds(x, 1), :] = perm[1, x, 0:1, :]
        ystage[0, 1, pl.ds(x, 1), :] = perm[1, x, dy - 1 : dy, :]
        return pack_into(packs, x, perm[2, x])

    packs = planes(first, zero_packs)
    for side, p in enumerate(packs):
        zstage[0, side] = p
    each(sends[1] + sends[2], start)
    pending += sends[0] + sends[1] + sends[2]

    shift_z, shift_c = dz.bit_length() - 1, column.bit_length() - 1
    own_rows = one_hot(cell >> shift_z, dx, F32)
    own_x3[...] = jnp.concatenate([own_rows] * 3, axis=0).astype(BF16)
    own_z[...] = one_hot(cell & (dz - 1), dz, BF16)
    own_col[...] = one_hot(remote & (column - 1), column, F32)
    near = scattered(weight, own_x3[...], own_z[...])

    def inner(x, carry):
        tx[x + 1] = harmonic(perm[0, x], perm[0, jnp.minimum(x + 1, dx - 1)])
        k = perm[1, x]
        ty[x] = jnp.where(row == dy - 1, 0.0, harmonic(k, pltpu.roll(k, dy - 1, 0)))
        k = perm[2, x]
        tz[x] = jnp.where(lane == dz - 1, 0.0, harmonic(k, pltpu.roll(k, dz - 1, 1)))
        return carry

    loads[6].wait()
    planes(inner, 0)

    def arrived(copy):
        copy.wait_recv()

    each(list_receives, arrived)
    far = 0.0
    for other in range(nz):
        up_cell = listland[other, 0:1, :].astype(jnp.int32)
        up_remote = listland[other, 1:2, :].astype(jnp.int32)
        up_weight = listland[other, 2:3, :]
        rows = one_hot(up_cell >> shift_z, dx, F32)
        up_x3[other] = jnp.concatenate([rows] * 3, axis=0).astype(BF16)
        up_z[other] = one_hot(up_cell & (dz - 1), dz, F32)
        up_own[other] = one_hot((up_remote & (column - 1)) - l * dz, dz, BF16)
        far = far + scattered(up_weight, up_x3[other], up_own[other])
    each(receives[0] + receives[1] + receives[2], arrived)
    for copy in loads[7:]:
        copy.wait()
    tx[0] = harmonic(perm[0, 0], xland[0, 0])
    tx[dx] = harmonic(perm[0, dx - 1], xland[0, 1])
    for side, extra in ((0, near), (1, far)):
        value = 0.0
        for other in range(nz):
            value = jnp.where(l == other, yland[0, side, other], value)
        t = harmonic(ystage[0, side], value)
        hyt[side] = t
        hy[side] = t + extra
    ztotal = []
    for side in range(len(z_sides)):
        t = jnp.where(lane < dx, harmonic(zstage[0, side], zland[0, side]), 0.0)
        hzt[side] = t
        ztotal.append(t)

    theta = (lam_high + lam_low) / 2.0
    delta = (lam_high - lam_low) / 2.0
    sigma = theta / delta

    def faced(x):
        return jnp.where(row == 0, hy[0, pl.ds(x, 1), :], 0.0) + jnp.where(
            row == dy - 1, hy[1, pl.ds(x, 1), :], 0.0
        )

    def rims(x, values):
        return faced(x) + unpacked(values, x)

    def put_rows(ref, x, plane):
        ref[0, pl.ds(x, 1), :] = plane[0:1, :]
        ref[1, pl.ds(x, 1), :] = plane[dy - 1 : dy, :]

    def begin(x, carry):
        packs, inv_packs = carry
        y, z = ty[x], tz[x]
        diagonal = acc[x] + (tx[x] + tx[x + 1]) + (y + pltpu.roll(y, 1, 0))
        diagonal = diagonal + (z + pltpu.roll(z, 1, 1)) + rims(x, ztotal)
        inverse = 1.0 / diagonal
        value = inverse * rhs[x]
        inv[x] = inverse
        g[x] = value
        value = value * (1.0 / theta)
        c0[x + 1] = value
        put_rows(ystage.at[1], x, value)
        put_rows(yinv, x, inverse)
        return pack_into(packs, x, value), pack_into(inv_packs, x, inverse)

    packs, inv_packs = planes(begin, (zero_packs, zero_packs))
    for side in range(len(z_sides)):
        zstage[1, side] = packs[side]
        zinv[side] = inv_packs[side]
    xstage[1, 0] = c0[1]
    xstage[1, 1] = c0[dx]
    for side, edge in ((0, 0), (1, dx)):
        hxt[side] = tx[edge]
        tx[edge] = jnp.zeros((dy, dz), F32)

    square = dz - 2 * dx
    sends, receives = copies(1, (xstage.at[1, 0], xstage.at[1, 1]))
    each(sends[1] + sends[2] + sends[0], start)
    pending += sends[0] + sends[1] + sends[2]
    now, before = c0, c1
    rho = 1.0 / sigma
    b = 0.0
    for e in range(1, SWEEPS):
        rho_next = 1.0 / (2.0 * sigma - rho)
        a, b_old, b = rho_next * rho, b, 2.0 * rho_next / delta
        rho = rho_next
        if e > 1:
            now[1] = xstage[e, 0]
            now[dx] = xstage[e, 1]

        def bulk(x, packs, fix, e=e, now=now, before=before, a=a, b=b, b_old=b_old):
            if fix and e > 1:
                values = [hz[side] for side in range(len(z_sides))]
                now[x + 2] = now[x + 2] + b_old * inv[x + 1] * rims(x + 1, values)
            v = now[x + 1]
            y, z = ty[x], tz[x]
            total = tx[x + 1] * now[x + 2] + tx[x] * now[x]
            total = total + (y * pltpu.roll(v, dy - 1, 0) + pltpu.roll(y * v, 1, 0))
            total = total + (z * pltpu.roll(v, dz - 1, 1) + pltpu.roll(z * v, 1, 1))
            new = (1.0 + a - b) * v + b * (g[x] + inv[x] * total)
            if e > 1:
                new = new - a * before[x + 1]
            before[x + 1] = new
            if e == SWEEPS - 1:
                return packs
            put_rows(ypart, x, new)
            return pack_into(packs, x, new)

        def group(step, packs, bulk=bulk):
            for u in range(UNROLL):
                packs = bulk(step * UNROLL + u, packs, True)
            return packs

        packs = lax.fori_loop(0, dx // UNROLL - 1, group, zero_packs)
        for x in range(dx - UNROLL, dx):
            packs = bulk(x, packs, x < dx - 2)

        each(receives[1], arrived)
        flux = 0.0
        far = 0.0
        sides = [0.0, 0.0]
        for other in range(nz):
            rows = slice(other * dz, (other + 1) * dz)
            flux = flux + gathered(yland[e, 0, other], own_x3[...], own_col[rows, :])
            up = listland[other, 2:3, :] * gathered(yland[e, 1, other], up_x3[other], up_z[other])
            far = far + scattered(up, up_x3[other], up_own[other])
            for side in range(2):
                sides[side] = jnp.where(l == other, yland[e, side, other], sides[side])
        near = scattered(weight * flux, own_x3[...], own_z[...])
        yvalues = [hyt[0] * sides[0] + near, hyt[1] * sides[1] + far]
        each(receives[2] + receives[0], arrived)
        for side in range(2):
            hy[side] = yvalues[side]
            hx[side] = hxt[side] * xland[e, side]
        zvalues = [hzt[side] * zland[e, side] for side in range(len(z_sides))]
        for side in range(len(z_sides)):
            hz[side] = zvalues[side]

        if e == SWEEPS - 1:
            ends = []
            for side, x in ((0, 0), (1, dx - 1)):
                ends.append(before[x + 1] + b * inv[x] * (hx[side] + rims(x, zvalues)))
            out[0] = ends[0]
            out[dx - 1] = ends[1]

            def last(x, carry, before=before, b=b):
                values = [hz[side] for side in range(len(z_sides))]
                out[x] = before[x + 1] + b * inv[x] * rims(x, values)
                return carry

            lax.fori_loop(1, dx - 1, last, 0)
            continue
        sends, receives = copies(e + 1, (xstage.at[e + 1, 0], xstage.at[e + 1, 1]))
        pending += sends[0] + sends[1] + sends[2]
        xrow = lax.broadcasted_iota(jnp.int32, (dx, dz), 0)
        xlane = lax.broadcasted_iota(jnp.int32, (dx, dz), 1)
        turned = [
            jnp.concatenate([v, jnp.zeros((dz - dy, dz), F32)], axis=0).T[0:dx, :]
            for v in zvalues
        ]
        for side, y in ((0, 0), (1, dy - 1)):
            term = yvalues[side]
            term = term + jnp.where(xrow == 0, hx[0, y : y + 1, :], 0.0)
            term = term + jnp.where(xrow == dx - 1, hx[1, y : y + 1, :], 0.0)
            for t, (edge, _, _, _) in zip(turned, z_sides):
                shifted = pltpu.roll(t, lax.rem(edge + dz - y, dz), 1)
                term = term + jnp.where(xlane == edge, shifted, 0.0)
            ystage[e + 1, side] = ypart[side] + b * yinv[side] * term
        each(sends[1], start)
        turn[...] = jnp.concatenate(yvalues + [jnp.zeros((square, dz), F32)], axis=0).T
        for (edge, _, _, zside), p in zip(z_sides, packs):
            line = turn[pl.ds(edge, 1), :]
            line = jnp.broadcast_to(line, (8, dz))
            upper = pltpu.roll(line, dz - dx, 1)
            term = zvalues[zside]
            term = term + jnp.where(row == 0, line[0:1, :], 0.0)
            term = term + jnp.where(row == dy - 1, upper[0:1, :], 0.0)
            for side, x in ((0, 0), (1, dx - 1)):
                shifted = pltpu.roll(hx[side], pack_shift(x, edge), 1)
                term = term + jnp.where(lane == x, shifted, 0.0)
            zstage[e + 1, zside] = p + b * zinv[zside] * term
        each(sends[2], start)
        ends = []
        for side, x in ((0, 0), (1, dx - 1)):
            ends.append(before[x + 1] + b * inv[x] * (hx[side] + rims(x, zvalues)))
        xstage[e + 1, 0] = ends[0]
        xstage[e + 1, 1] = ends[1]
        each(sends[0], start)
        now, before = before, now
    each(pending, lambda copy: copy.wait_send())


def local(sizes, rhs, accumulation, permeability, nnc_cell, nnc_remote, nnc_mask, nnc_trans):
    nx, ny, nz = sizes
    dx, dy, dz = rhs.shape
    slots = nnc_cell.shape[-1]
    column = dz * nz
    plane = (dx, dy, dz)
    zn = 1 if nz == 2 else 2
    vmem = pl.BlockSpec(memory_space=pltpu.VMEM)
    hbm = pl.BlockSpec(memory_space=pltpu.HBM)
    dma = pltpu.SemaphoreType.DMA
    V = pltpu.VMEM
    scratch = [
        V(plane, F32), V(plane, F32), V((3, *plane), F32),
        V((1, slots), jnp.int32), V((1, slots), jnp.int32), V((1, slots), jnp.int32),
        V((1, slots), F32), dma((9,)),
        V((dx + 2, dy, dz), F32), V((dx + 2, dy, dz), F32),
        V(plane, F32), V(plane, F32),
        V((dx + 1, dy, dz), F32), V(plane, F32), V(plane, F32),
        V((2, dy, dz), F32), V((2, dy, dz), F32), V((2, dx, dz), F32), V((2, dx, dz), F32),
        V((zn, dy, dz), F32), V((zn, dy, dz), F32),
        V((2, dx, dz), F32), V((zn, dy, dz), F32), V((2, dx, dz), F32), V((dz, dz), F32),
        V((SWEEPS, 2, dy, dz), F32),
        V((SWEEPS, 2, dx, dz), F32), V((SWEEPS, zn, dy, dz), F32),
        V((SWEEPS, 2, dy, dz), F32), V((SWEEPS, 2, nz, dx, dz), F32),
        V((SWEEPS, zn, dy, dz), F32),
        V((8, slots), F32), V((nz, 8, slots), F32),
        V((3 * dx, slots), BF16), V((dz, slots), BF16), V((column, slots), F32),
        V((nz, 3 * dx, slots), BF16), V((nz, dz, slots), F32), V((nz, dz, slots), BF16),
        dma((SWEEPS, 2)), dma((SWEEPS, 2)),
        dma((SWEEPS, 2, nz)), dma((SWEEPS, 2, nz)),
        dma((SWEEPS, zn)), dma((SWEEPS, zn)),
        dma((nz,)), dma((nz,)),
    ]
    return pl.pallas_call(
        functools.partial(kernel, sizes),
        out_shape=jax.ShapeDtypeStruct(plane, F32),
        in_specs=[hbm] * 7,
        out_specs=vmem,
        scratch_shapes=scratch,
        compiler_params=pltpu.CompilerParams(
            collective_id=0, has_side_effects=True, vmem_limit_bytes=48 * 1024 * 1024
        ),
    )(
        rhs, accumulation, permeability,
        *(v.reshape(1, slots) for v in (nnc_cell, nnc_remote, nnc_mask, nnc_trans)),
    )


def solution(mesh):
    sizes = tuple(mesh.shape[name] for name in ("gx", "gy", "gz"))
    cells = P("gx", "gy", "gz")
    lists = P("gx", "gy", "gz", None)
    return jax.shard_map(
        functools.partial(local, sizes),
        mesh=mesh,
        in_specs=(cells, cells, P(None, "gx", "gy", "gz"), lists, lists, lists, lists),
        out_specs=cells,
        check_vma=False,
    )
```
